32 devices in a mesh: parts: 2 (over y), section: 4 (over z), seq: 2 (over core), tensor: 2 (over x).
Axes of the slice: x: 2, y: 2, z: 4, core: 2. Of those that a mesh axis runs over, the one named last changes fastest.
Arguments:
- hidden_state: bfloat16 [8, 1024, 5120], P(('parts', 'section'), 'seq', 'tensor'), parts along dimension 0, may hold values from -6 to 6
- frame_query: bfloat16 [8, 1024, 2560], P(('parts', 'section'), 'seq', 'tensor'), parts along dimension 0, may hold values from -12 to 12
- frame_key: bfloat16 [8, 1024, 2560], P(('parts', 'section'), 'seq', 'tensor'), parts along dimension 0, may hold values from -6 to 6
- frame_value: bfloat16 [8, 1024, 2560], P(('parts', 'section'), 'seq', 'tensor'), parts along dimension 0, may hold values from -6 to 6
- cache_key: bfloat16 [2048, 2560], P(('parts', 'section', 'seq'), 'tensor'), parts along dimension 0, may hold values from -6 to 6
- cache_value: bfloat16 [2048, 2560], P(('parts', 'section', 'seq'), 'tensor'), parts along dimension 0, may hold values from -6 to 6
- out_weight: bfloat16 [2560, 5120], P('tensor'), may hold values from -0.8984375 to 0.8984375
- level_gate: float32 [8, 5120], P(None, 'tensor'), may hold values from 0.5 to 1.5
- noise_level: int32 [8], P('parts'), parts along dimension 0, may hold values from 0 to 7
- frame_position: int32 [8], P('parts'), parts along dimension 0, may hold values from 0 to 3, each once
- cached_count: int32 [2], P('parts'), parts along dimension 0, may hold values from 256 to 1024
Outputs:
- advanced: bfloat16 [8, 1024, 5120], P(('parts', 'section'), 'seq', 'tensor'), parts along dimension 0
The draws below stay inside these ranges and needn't reach their ends.
There are 2 independent parts, one for each index of `parts`. The reference program is written for one: setup_inputs(seed, part) draws one part's arguments, and reference() takes and returns one part's arrays. A program takes and returns all parts, laid end to end along the dimension named above; an argument that names none is the same for every part. Nothing has to cross between parts.
Inputs may be any that keep to these rules, and one draw needn't show every extreme that they name: `frame_position`: a permutation: every section holds a different frame position.
All inputs are finite; a program needn't handle non-finite values.
Results may differ from the reference program's by a relative error of at most 0.015.
Values may be sent and summed in bfloat16 or wider, within the bound.
A program may use at most 128 MiB of HBM per device.

```python
import jax
import jax.numpy as jnp
from jax import lax

D = 5120
HEADS = 20
HD = 128
LEVELS = 8
FTOK = 1024
CROWS = 256
N_SECTION = 4
N_TENSOR = 2


def draw_frame_query(key, part):
    key = jax.random.fold_in(key, 11)
    shape = (N_SECTION, FTOK, HEADS * HD)
    return jnp.clip(2.0 * jax.random.normal(key, shape, jnp.float32), -12.0, 12.0).astype(jnp.bfloat16)


def draw_frame_key(key, part):
    key = jax.random.fold_in(key, 23)
    shape = (N_SECTION, FTOK, HEADS * HD)
    return jnp.clip(jax.random.normal(key, shape, jnp.float32), -6.0, 6.0).astype(jnp.bfloat16)


def touch_ends(values, stream_key, low, top_value):
    dims = values.shape
    index_at = [jax.random.randint(jax.random.fold_in(stream_key, axis), (), 0, dims[axis]) for axis in range(len(dims))]
    values = values.at[tuple(index_at)].set(low)
    longest = dims.index(max(dims))
    index_at[longest] = (index_at[longest] + 1) % dims[longest]
    return values.at[tuple(index_at)].set(top_value)


def level_of(rng, dims, cuts, low, high):
    def one(dim, parts):
        steps = jax.random.uniform(jax.random.fold_in(jax.random.fold_in(rng, 6), dim), (parts,), jnp.float32, low / len(cuts), high / len(cuts))
        return jnp.repeat(jnp.exp(steps), dims[dim] // parts).reshape((-1,) + (1,) * (len(dims) - dim - 1))

    gain = one(*cuts[0])
    for cut in cuts[1:]:
        gain = gain * one(*cut)
    return gain


def gaussian(own_key, extent, deviation, most, cuts=(), kind=jnp.bfloat16):
    result = deviation * jax.random.normal(own_key, extent, jnp.float32)
    if cuts:
        result = result * level_of(own_key, extent, cuts, -0.22, 0.18)
    return jnp.clip(result, -most, most).astype(kind)


def setup_inputs(seed: int = 0, part: int = 0) -> dict:
    splits = jax.random.split(jax.random.key(seed), 12)
    part_splits = jax.random.split(jax.random.fold_in(splits[11], part), 12)
    hidden_state = gaussian(part_splits[0], (N_SECTION, FTOK, D), 1.0, 6.0, ((0, 4), (1, 2), (2, 2)))
    frame_query = draw_frame_query(jax.random.fold_in(jax.random.fold_in(splits[11], part), 71), part)
    frame_key = draw_frame_key(jax.random.fold_in(jax.random.fold_in(splits[11], part), 71), part)
    frame_value = gaussian(part_splits[3], (N_SECTION, FTOK, HEADS * HD), 1.0, 6.0, ((0, 4), (1, 2), (2, 2)))
    cache_key = gaussian(part_splits[4], (N_SECTION * CROWS, HEADS * HD), 1.0, 6.0, ((0, 8), (1, 2)))
    cache_value = gaussian(part_splits[5], (N_SECTION * CROWS, HEADS * HD), 1.0, 6.0, ((0, 8), (1, 2)))
    out_weight = gaussian(splits[6], (HEADS * HD, D), 0.15, 0.8984375, ((0, 2),))
    level_gate = jnp.clip(0.5 + 1.0 * jax.random.uniform(splits[7], (LEVELS, D), jnp.float32) ** level_of(splits[7], (LEVELS, D), ((1, 2),), -0.2, 0.2), 0.5, 1.5)
    noise_level = touch_ends(jax.random.randint(part_splits[8], (N_SECTION,), 0, LEVELS), jax.random.fold_in(part_splits[8], 1), 0, LEVELS - 1).astype(jnp.int32)
    frame_position = jax.random.permutation(part_splits[9], N_SECTION).astype(jnp.int32)
    cached_count = jax.random.randint(part_splits[10], (1,), N_SECTION * CROWS // 4, N_SECTION * CROWS + 1).astype(jnp.int32)
    return dict(hidden_state=hidden_state, frame_query=frame_query, frame_key=frame_key, frame_value=frame_value, cache_key=cache_key, cache_value=cache_value, out_weight=out_weight, level_gate=level_gate, noise_level=noise_level, frame_position=frame_position, cached_count=cached_count)


def reference(hidden_state, frame_query, frame_key, frame_value, cache_key, cache_value, out_weight, level_gate, noise_level, frame_position, cached_count):
    cache_total = N_SECTION * CROWS
    row_index = jnp.arange(cache_total, dtype=jnp.int32)
    slot_index = row_index // CROWS
    group_cols = HEADS * HD // N_TENSOR
    cache_keys = cache_key.astype(jnp.float32).reshape(cache_total, HEADS, HD)
    cache_values = cache_value.astype(jnp.float32).reshape(cache_total, HEADS, HD)
    out_groups = out_weight.astype(jnp.float32).reshape(N_TENSOR, group_cols, D)

    def one_section(section):
        visible = (row_index < cached_count[0]) & (slot_index < frame_position[section])
        allowed = jnp.concatenate([jnp.ones((FTOK,), dtype=bool), visible])
        queries = frame_query[section].astype(jnp.float32).reshape(FTOK, HEADS, HD)
        key_rows = jnp.concatenate([frame_key[section].astype(jnp.float32).reshape(FTOK, HEADS, HD), cache_keys], 0)
        value_rows = jnp.concatenate([frame_value[section].astype(jnp.float32).reshape(FTOK, HEADS, HD), cache_values], 0)
        scores = jnp.einsum("thd,nhd->thn", queries, key_rows) * (HD ** -0.5)
        scores = jnp.where(allowed[None, None, :], scores, -1.0e30)
        highest = jnp.max(scores, axis=2, keepdims=True)
        exponent = jnp.exp(scores - highest)
        weights = (exponent / jnp.sum(exponent, axis=2, keepdims=True)).astype(jnp.bfloat16)
        weights = lax.optimization_barrier(weights)
        attended = jnp.einsum("thn,nhd->thd", weights.astype(jnp.float32), value_rows).astype(jnp.bfloat16)
        attended = lax.optimization_barrier(attended)
        grouped = attended.astype(jnp.float32).reshape(FTOK, N_TENSOR, group_cols)
        partial_value = jnp.einsum("tgc,gcd->gtd", grouped, out_groups).astype(jnp.bfloat16)
        partial_value = lax.optimization_barrier(partial_value)
        branch_sum = jnp.sum(partial_value.astype(jnp.float32), axis=0)
        gate_row = level_gate[noise_level[section]]
        return (hidden_state[section].astype(jnp.float32) + gate_row[None, :] * branch_sum).astype(jnp.bfloat16)

    updated = lax.map(one_section, jnp.arange(N_SECTION, dtype=jnp.int32))
    return jnp.roll(updated, 1, axis=0)
```

```python
import functools
import math

import jax
import jax.numpy as jnp
from jax import lax
from jax.experimental import pallas as pl
from jax.experimental.pallas import tpu as pltpu
from jax.sharding import PartitionSpec as P

HD = 128
MESH = pl.DeviceIdType.MESH
hidden_score = -1e30
to_power = HD ** (-0.5) * math.log2(math.e)
row_chunks = 4
column_parts = 2


def scores_of(queries, keys):
    return lax.dot_general(
        queries, keys, (((1,), (1,)), ((), ())), preferred_element_type=jnp.float32
    )


def weighted(scores, top, values):
    weights = jnp.exp2((scores - top) * to_power).astype(jnp.bfloat16)
    with_ones = jnp.concatenate([values, jnp.ones_like(values)], axis=1)
    return jnp.dot(weights, with_ones, preferred_element_type=jnp.float32)


def kernel(
    sections,
    tensors,
    noise_ref,
    position_ref,
    count_ref,
    query,
    key,
    value,
    cache_key,
    cache_value,
    level_gate,
    weight_hbm,
    hidden_hbm,
    out,
    key_other,
    value_other,
    cache_keys,
    cache_values,
    weight,
    hidden,
    running,
    highest,
    bias,
    gate,
    attended,
    partial_out,
    partial_in,
    partial_own,
    updated,
    local_sem,
    frame_send,
    frame_recv,
    right_send,
    left_send,
    line_recv,
    pair_send,
    pair_recv,
    partial_send,
    partial_recv,
    shift_send,
    shift_recv,
):
    me = lax.axis_index("section")
    core = lax.axis_index("seq")
    group = lax.axis_index("tensor")
    after = lax.rem(me + 1, sections)
    before = lax.rem(me + sections - 1, sections)
    tokens = query.shape[0]
    heads = query.shape[1] // HD
    half_rows = cache_key.shape[0]
    slot_rows = 2 * half_rows
    used = sections - 1
    width = level_gate.shape[1]
    part_width = width // column_parts
    chunk = tokens // row_chunks

    barrier = pltpu.get_barrier_semaphore()
    peers = [{"seq": 1 - core}, {"section": after}, {"section": before}]
    peers += [{"tensor": lax.rem(group + d, tensors)} for d in range(1, tensors)]
    for peer in peers:
        pl.semaphore_signal(barrier, inc=1, device_id=peer, device_id_type=MESH)

    weight_copy = pltpu.make_async_copy(weight_hbm, weight, local_sem.at[0])
    hidden_copy = pltpu.make_async_copy(hidden_hbm.at[0], hidden, local_sem.at[1])
    own_rows = pl.ds(pl.multiple_of(me * slot_rows + core * half_rows, half_rows), half_rows)

    @pl.when(me < used)
    def _():
        cache_keys[own_rows, :] = cache_key[...]
        cache_values[own_rows, :] = cache_value[...]

    pl.semaphore_wait(barrier, len(peers))

    def line_copies(slot, sends, target):
        rows = pl.ds(pl.multiple_of(slot * slot_rows + core * half_rows, half_rows), half_rows)
        return [
            pltpu.make_async_remote_copy(
                src_ref=rows_of.at[rows],
                dst_ref=rows_of.at[rows],
                send_sem=sends.at[which, slot],
                recv_sem=(pair_recv if sends is pair_send else line_recv).at[which, slot],
                device_id=target,
                device_id_type=MESH,
            )
            for which, rows_of in enumerate((cache_keys, cache_values))
        ]

    def to_right(slot):
        return line_copies(slot, right_send, {"section": after})

    def to_left(slot):
        return line_copies(slot, left_send, {"section": before})

    def to_pair(slot):
        return line_copies(slot, pair_send, {"seq": 1 - core})

    def start(copies):
        for copy in copies:
            copy.start()

    def pair_arrived(slot):
        rows = pl.ds(
            pl.multiple_of(slot * slot_rows + (1 - core) * half_rows, half_rows), half_rows
        )
        for which, rows_of in enumerate((cache_keys, cache_values)):
            pltpu.make_async_remote_copy(
                src_ref=rows_of.at[rows],
                dst_ref=rows_of.at[rows],
                send_sem=pair_send.at[which, slot],
                recv_sem=pair_recv.at[which, slot],
                device_id={"seq": 1 - core},
                device_id_type=MESH,
            ).wait_recv()

    frame_copies = [
        pltpu.make_async_remote_copy(
            src_ref=source,
            dst_ref=landing,
            send_sem=frame_send.at[which],
            recv_sem=frame_recv.at[which],
            device_id={"seq": 1 - core},
            device_id_type=MESH,
        )
        for which, (source, landing) in enumerate(((key, key_other), (value, value_other)))
    ]

    @pl.when(me < used)
    def _():
        start(to_right(me))

    @pl.when((me >= 1) & (me < used))
    def _():
        start(to_left(me))

    start(frame_copies)

    @pl.when(me < used)
    def _():
        start(to_pair(me))

    weight_copy.start()
    hidden_copy.start()

    def relay(step, carry):
        from_left = me - 1 - step
        from_right = me + 1 + step

        @pl.when(from_left >= 0)
        def _():
            for copy in to_right(from_left):
                copy.wait_recv()

            @pl.when(me < used)
            def _():
                start(to_right(from_left))

            start(to_pair(from_left))

        @pl.when(from_right < used)
        def _():
            for copy in to_left(from_right):
                copy.wait_recv()

            @pl.when(me >= 1)
            def _():
                start(to_left(from_right))

            start(to_pair(from_right))

        return carry

    limit = jnp.minimum(count_ref[0], position_ref[me] * slot_rows)
    row = lax.broadcasted_iota(jnp.int32, bias.shape, 1)
    bias[...] = jnp.where(row < limit, 0.0, hidden_score)
    level = lax.broadcasted_iota(jnp.int32, level_gate.shape, 0)
    gate[...] = jnp.sum(
        jnp.where(level == noise_ref[me], level_gate[...], 0.0), axis=0, keepdims=True
    )

    for copy in frame_copies:
        copy.wait_recv()
    block = min(tokens, 256)

    def frame_head(h, carry):
        columns = pl.ds(pl.multiple_of(h * HD, HD), HD)
        for first in range(0, tokens, block):
            rows = pl.ds(first, block)
            queries = query[rows, columns]
            near = scores_of(queries, key[:, columns])
            far = scores_of(queries, key_other[:, columns])
            top = jnp.max(jnp.maximum(near, far), axis=1, keepdims=True)
            running[h, rows, :] = weighted(near, top, value[:, columns]) + weighted(
                far, top, value_other[:, columns]
            )
            highest[h, rows, :] = jnp.broadcast_to(top, (block, HD))
        return carry

    early = max(1, (heads * 7) // 10)
    lax.fori_loop(0, early, frame_head, 0)
    relay(0, 0)
    lax.fori_loop(early, heads, frame_head, 0)
    lax.fori_loop(1, used, relay, 0)

    def slot_ready(slot, carry):
        pair_arrived(slot)
        return carry

    lax.fori_loop(0, used, slot_ready, 0)
    weight_copy.wait()
    hidden_copy.wait()

    def partial_copy(d, unit):
        return pltpu.make_async_remote_copy(
            src_ref=partial_out.at[d - 1, unit],
            dst_ref=partial_in.at[d - 1, unit],
            send_sem=partial_send.at[d - 1, unit],
            recv_sem=partial_recv.at[d - 1, unit],
            device_id={"tensor": lax.rem(group + d, tensors)},
            device_id_type=MESH,
        )

    def shift_copy(c, part):
        unit = c * column_parts + part
        rows = pl.ds(pl.multiple_of(c * chunk, chunk), chunk)
        return pltpu.make_async_remote_copy(
            src_ref=updated.at[unit],
            dst_ref=out.at[0, rows, pl.ds(part * part_width, part_width)],
            send_sem=shift_send.at[unit],
            recv_sem=shift_recv.at[unit],
            device_id={"section": after},
            device_id_type=MESH,
        )

    def combine(c):
        rows = pl.ds(pl.multiple_of(c * chunk, chunk), chunk)
        for part in range(column_parts):
            unit = c * column_parts + part
            columns = pl.ds(part * part_width, part_width)
            branch = partial_own[unit].astype(jnp.float32)
            for d in range(1, tensors):
                partial_copy(d, unit).wait_recv()
                branch = branch + partial_in[d - 1, unit].astype(jnp.float32)
            updated[unit] = (
                hidden[rows, columns].astype(jnp.float32) + gate[:, columns] * branch
            ).astype(jnp.bfloat16)
            shift_copy(c, part).start()

    def row_step(c, carry):
        rows = pl.ds(pl.multiple_of(c * chunk, chunk), chunk)

        def cache_head(h, inner):
            columns = pl.ds(pl.multiple_of(h * HD, HD), HD)
            scores = scores_of(query[rows, columns], cache_keys[:, columns]) + bias[...]
            old_top = highest[h, rows, :]
            top = jnp.maximum(old_top, jnp.max(scores, axis=1, keepdims=True))
            factor = jnp.exp2((old_top - top) * to_power)
            total = weighted(scores, top[:, :1], cache_values[:, columns])
            old = running[h, rows, :]
            summed = old[:, :HD] * factor + total[:, :HD]
            weight_sum = old[:, HD:] * factor + total[:, HD:]
            attended[:, columns] = (summed / weight_sum).astype(jnp.bfloat16)
            return inner

        lax.fori_loop(0, heads, cache_head, 0)

        def project(owner, part):
            columns = pl.ds(pl.multiple_of(owner * width + part * part_width, HD), part_width)
            return jnp.dot(
                attended[...], weight[:, columns], preferred_element_type=jnp.float32
            ).astype(jnp.bfloat16)

        for part in range(column_parts):
            unit = c * column_parts + part
            for d in range(1, tensors):
                partial_out[d - 1, unit] = project(lax.rem(group + d, tensors), part)
                partial_copy(d, unit).start()
        for part in range(column_parts):
            partial_own[c * column_parts + part] = project(group, part)

        @pl.when(c >= 1)
        def _():
            combine(c - 1)

        return carry

    lax.fori_loop(0, row_chunks, row_step, 0)
    combine(row_chunks - 1)

    for copy in frame_copies:
        copy.wait_send()

    def slot_sent(slot, carry):
        @pl.when((slot <= me) & (me < used))
        def _():
            for copy in to_right(slot):
                copy.wait_send()

        @pl.when((slot >= me) & (me >= 1))
        def _():
            for copy in to_left(slot):
                copy.wait_send()

        for copy in to_pair(slot):
            copy.wait_send()
        return carry

    lax.fori_loop(0, used, slot_sent, 0)

    def chunk_done(c, carry):
        for part in range(column_parts):
            for d in range(1, tensors):
                partial_copy(d, c * column_parts + part).wait_send()
            shift_copy(c, part).wait()
        return carry

    lax.fori_loop(0, row_chunks, chunk_done, 0)


def on_device(
    hidden_state,
    frame_query,
    frame_key,
    frame_value,
    cache_key,
    cache_value,
    out_weight,
    level_gate,
    noise_level,
    frame_position,
    cached_count,
):
    sections = lax.axis_size("section")
    tensors = lax.axis_size("tensor")
    tokens, inner = frame_query.shape[1:]
    heads = inner // HD
    width = hidden_state.shape[2]
    used_rows = (sections - 1) * 2 * cache_key.shape[0]
    units = row_chunks * column_parts
    chunk = tokens // row_chunks
    piece = (chunk, width // column_parts)
    bf16, f32 = jnp.bfloat16, jnp.float32
    scalars = pl.BlockSpec(memory_space=pltpu.SMEM)
    near = pl.BlockSpec(memory_space=pltpu.VMEM)
    far = pl.BlockSpec(memory_space=pl.ANY)
    dma = pltpu.SemaphoreType.DMA
    return pl.pallas_call(
        functools.partial(kernel, sections, tensors),
        out_shape=jax.ShapeDtypeStruct(hidden_state.shape, bf16),
        in_specs=[scalars] * 3 + [near] * 6 + [far] * 2,
        out_specs=far,
        scratch_shapes=[
            pltpu.VMEM((tokens, inner), bf16),
            pltpu.VMEM((tokens, inner), bf16),
            pltpu.VMEM((used_rows, inner), bf16),
            pltpu.VMEM((used_rows, inner), bf16),
            pltpu.VMEM(out_weight.shape, bf16),
            pltpu.VMEM((tokens, width), bf16),
            pltpu.VMEM((heads, tokens, 2 * HD), f32),
            pltpu.VMEM((heads, tokens, HD), f32),
            pltpu.VMEM((1, used_rows), f32),
            pltpu.VMEM((1, width), f32),
            pltpu.VMEM((chunk, inner), bf16),
            pltpu.VMEM((tensors - 1, units) + piece, bf16),
            pltpu.VMEM((tensors - 1, units) + piece, bf16),
            pltpu.VMEM((units,) + piece, bf16),
            pltpu.VMEM((units,) + piece, bf16),
            dma((2,)),
            dma((2,)),
            dma((2,)),
            dma((2, sections - 1)),
            dma((2, sections - 1)),
            dma((2, sections - 1)),
            dma((2, sections - 1)),
            dma((2, sections - 1)),
            dma((tensors - 1, units)),
            dma((tensors - 1, units)),
            dma((units,)),
            dma((units,)),
        ],
        compiler_params=pltpu.CompilerParams(
            collective_id=0, has_side_effects=True, vmem_limit_bytes=60 * 1024 * 1024
        ),
    )(
        noise_level,
        frame_position,
        cached_count,
        frame_query[0],
        frame_key[0],
        frame_value[0],
        cache_key,
        cache_value,
        level_gate,
        out_weight,
        hidden_state,
    )


def solution(mesh):
    placed = (
        P(("parts", "section"), "seq", "tensor"),
        P(("parts", "section"), "seq", "tensor"),
        P(("parts", "section"), "seq", "tensor"),
        P(("parts", "section"), "seq", "tensor"),
        P(("parts", "section", "seq"), "tensor"),
        P(("parts", "section", "seq"), "tensor"),
        P("tensor", None),
        P(None, "tensor"),
        P("parts"),
        P("parts"),
        P("parts"),
    )
    return jax.shard_map(
        on_device,
        mesh=mesh,
        in_specs=placed,
        out_specs=P(("parts", "section"), "seq", "tensor"),
        check_vma=False,
    )
```

```python
import functools
import math

import jax
import jax.numpy as jnp
from jax import lax
from jax.experimental import pallas as pl
from jax.experimental.pallas import tpu as pltpu
from jax.sharding import PartitionSpec as P

HD = 128
MESH = pl.DeviceIdType.MESH
hidden_score = -1e30
to_power = HD ** (-0.5) * math.log2(math.e)
row_chunks = 4
column_parts = 5
lag = 2


def scores_of(queries, keys):
    return lax.dot_general(
        queries, keys, (((1,), (1,)), ((), ())), preferred_element_type=jnp.float32
    )


def weighted(scores, top, values):
    weights = jnp.exp2((scores - top) * to_power).astype(jnp.bfloat16)
    with_ones = jnp.concatenate([values, jnp.ones_like(values)], axis=1)
    return jnp.dot(weights, with_ones, preferred_element_type=jnp.float32)


def kernel(
    sections,
    tensors,
    noise_ref,
    position_ref,
    count_ref,
    query,
    key,
    value,
    cache_key,
    cache_value,
    level_gate,
    weight_hbm,
    hidden_hbm,
    out,
    key_other,
    value_other,
    cache_keys,
    cache_values,
    weight,
    hidden,
    running,
    highest,
    gate,
    attended,
    partial_out,
    partial_in,
    partial_own,
    updated,
    local_sem,
    frame_send,
    frame_recv,
    right_send,
    left_send,
    line_recv,
    pair_send,
    pair_recv,
    partial_send,
    partial_recv,
    shift_send,
    shift_recv,
):
    me = lax.axis_index("section")
    core = lax.axis_index("seq")
    group = lax.axis_index("tensor")
    after = lax.rem(me + 1, sections)
    before = lax.rem(me + sections - 1, sections)
    tokens = query.shape[0]
    heads = query.shape[1] // HD
    half_rows = cache_key.shape[0]
    slot_rows = 2 * half_rows
    used = sections - 1
    width = level_gate.shape[1]
    part_width = width // column_parts
    chunk = tokens // row_chunks

    barrier = pltpu.get_barrier_semaphore()
    peers = [{"seq": 1 - core}, {"section": after}, {"section": before}]
    peers += [{"tensor": lax.rem(group + d, tensors)} for d in range(1, tensors)]
    for peer in peers:
        pl.semaphore_signal(barrier, inc=1, device_id=peer, device_id_type=MESH)

    weight_copy = pltpu.make_async_copy(weight_hbm, weight, local_sem.at[0])
    hidden_copy = pltpu.make_async_copy(hidden_hbm.at[0], hidden, local_sem.at[1])
    own_rows = pl.ds(pl.multiple_of(me * slot_rows + core * half_rows, half_rows), half_rows)

    @pl.when(me < used)
    def _():
        cache_keys[own_rows, :] = cache_key[...]
        cache_values[own_rows, :] = cache_value[...]

    pl.semaphore_wait(barrier, len(peers))

    def line_copy(slot, which, sends, target):
        rows = pl.ds(pl.multiple_of(slot * slot_rows + core * half_rows, half_rows), half_rows)
        rows_of = (cache_keys, cache_values)[which]
        return pltpu.make_async_remote_copy(
            src_ref=rows_of.at[rows],
            dst_ref=rows_of.at[rows],
            send_sem=sends.at[which, slot],
            recv_sem=(pair_recv if sends is pair_send else line_recv).at[which, slot],
            device_id=target,
            device_id_type=MESH,
        )

    def to_right(slot, kinds=(0, 1)):
        return [line_copy(slot, which, right_send, {"section": after}) for which in kinds]

    def to_left(slot, kinds=(0, 1)):
        return [line_copy(slot, which, left_send, {"section": before}) for which in kinds]

    def to_pair(slot, kinds=(0, 1)):
        return [line_copy(slot, which, pair_send, {"seq": 1 - core}) for which in kinds]

    def start(copies):
        for copy in copies:
            copy.start()

    def pair_arrived(slot):
        rows = pl.ds(
            pl.multiple_of(slot * slot_rows + (1 - core) * half_rows, half_rows), half_rows
        )
        for which, rows_of in enumerate((cache_keys, cache_values)):
            pltpu.make_async_remote_copy(
                src_ref=rows_of.at[rows],
                dst_ref=rows_of.at[rows],
                send_sem=pair_send.at[which, slot],
                recv_sem=pair_recv.at[which, slot],
                device_id={"seq": 1 - core},
                device_id_type=MESH,
            ).wait_recv()

    frame_copies = [
        pltpu.make_async_remote_copy(
            src_ref=source,
            dst_ref=landing,
            send_sem=frame_send.at[which],
            recv_sem=frame_recv.at[which],
            device_id={"seq": 1 - core},
            device_id_type=MESH,
        )
        for which, (source, landing) in enumerate(((key, key_other), (value, value_other)))
    ]

    @pl.when(me < used)
    def _():
        start(to_right(me))

    @pl.when((me >= 1) & (me < used))
    def _():
        start(to_left(me))

    start(frame_copies)

    @pl.when(me < used)
    def _():
        start(to_pair(me))

    weight_copy.start()
    hidden_copy.start()

    def relay(step, which):
        from_left = me - 1 - step
        from_right = me + 1 + step

        @pl.when(from_left >= 0)
        def _():
            to_right(from_left, (which,))[0].wait_recv()

            @pl.when(me < used)
            def _():
                start(to_right(from_left, (which,)))

            start(to_pair(from_left, (which,)))

        @pl.when(from_right < used)
        def _():
            to_left(from_right, (which,))[0].wait_recv()

            @pl.when(me >= 1)
            def _():
                start(to_left(from_right, (which,)))

            start(to_pair(from_right, (which,)))

    limit = jnp.minimum(count_ref[0], position_ref[me] * slot_rows)
    row = lax.broadcasted_iota(jnp.int32, (1, slot_rows), 1)
    level = lax.broadcasted_iota(jnp.int32, level_gate.shape, 0)
    gate[...] = jnp.sum(
        jnp.where(level == noise_ref[me], level_gate[...], 0.0), axis=0, keepdims=True
    )

    block = min(tokens, 256)

    def near_head(h, carry):
        columns = pl.ds(pl.multiple_of(h * HD, HD), HD)
        for first in range(0, tokens, block):
            rows = pl.ds(first, block)
            scores = scores_of(query[rows, columns], key[:, columns])
            top = jnp.max(scores, axis=1, keepdims=True)
            running[h, rows, :] = weighted(scores, top, value[:, columns])
            highest[h, rows, :] = jnp.broadcast_to(top, (block, HD))
        return carry

    def merged(scores, values, h, rows):
        old_top = highest[h, rows, :]
        top = jnp.maximum(old_top, jnp.max(scores, axis=1, keepdims=True))
        factor = jnp.exp2((old_top - top) * to_power)
        total = weighted(scores, top[:, :1], values)
        old = running[h, rows, :]
        return (
            old[:, :HD] * factor + total[:, :HD],
            old[:, HD:] * factor + total[:, HD:],
            top,
        )

    def keep(state, h, rows):
        running[h, rows, :] = jnp.concatenate(state[:2], axis=1)
        highest[h, rows, :] = state[2]

    def far_head(h, carry):
        columns = pl.ds(pl.multiple_of(h * HD, HD), HD)
        for first in range(0, tokens, block):
            rows = pl.ds(first, block)
            scores = scores_of(query[rows, columns], key_other[:, columns])
            keep(merged(scores, value_other[:, columns], h, rows), h, rows)
        return carry

    def with_slot(slot, h, rows):
        columns = pl.ds(pl.multiple_of(h * HD, HD), HD)
        slot_at = pl.ds(pl.multiple_of(slot * slot_rows, slot_rows), slot_rows)
        bias = jnp.where(row < limit - slot * slot_rows, 0.0, hidden_score)
        scores = scores_of(query[rows, columns], cache_keys[slot_at, columns]) + bias
        return merged(scores, cache_values[slot_at, columns], h, rows)

    final = jnp.where(2 * me >= used - 1, 0, used - 1)

    def take_slot(slot):
        @pl.when((slot >= 0) & (slot < used) & (slot != final))
        def _():
            pair_arrived(slot)

            def slot_head(h, carry):
                for first in range(0, tokens, block):
                    rows = pl.ds(first, block)
                    keep(with_slot(slot, h, rows), h, rows)
                return carry

            lax.fori_loop(0, heads, slot_head, 0)

    def slot_step(step, carry):
        relay(step, 0)
        take_slot(me - step)
        relay(step, 1)
        take_slot(me + step)
        return carry

    early = max(1, (heads * 2) // 5)
    lax.fori_loop(0, heads, near_head, 0)
    relay(0, 0)
    for copy in frame_copies:
        copy.wait_recv()
    lax.fori_loop(0, early, far_head, 0)
    relay(0, 1)
    lax.fori_loop(early, heads, far_head, 0)
    take_slot(me)
    lax.fori_loop(1, used, slot_step, 0)
    take_slot(me - used)
    take_slot(me + used)
    pair_arrived(final)
    weight_copy.wait()
    hidden_copy.wait()

    def partial_copy(d, unit):
        return pltpu.make_async_remote_copy(
            src_ref=partial_out.at[d - 1, unit],
            dst_ref=partial_in.at[d - 1, unit],
            send_sem=partial_send.at[d - 1, unit],
            recv_sem=partial_recv.at[d - 1, unit],
            device_id={"tensor": lax.rem(group + d, tensors)},
            device_id_type=MESH,
        )

    def shift_copy(c, part):
        unit = c * column_parts + part
        rows = pl.ds(pl.multiple_of(c * chunk, chunk), chunk)
        return pltpu.make_async_remote_copy(
            src_ref=updated.at[unit],
            dst_ref=out.at[0, rows, pl.ds(part * part_width, part_width)],
            send_sem=shift_send.at[unit],
            recv_sem=shift_recv.at[unit],
            device_id={"section": after},
            device_id_type=MESH,
        )

    def combine(c, part):
        rows = pl.ds(pl.multiple_of(c * chunk, chunk), chunk)
        unit = c * column_parts + part
        columns = pl.ds(part * part_width, part_width)
        branch = partial_own[unit].astype(jnp.float32)
        for d in range(1, tensors):
            partial_copy(d, unit).wait_recv()
            branch = branch + partial_in[d - 1, unit].astype(jnp.float32)
        updated[unit] = (
            hidden[rows, columns].astype(jnp.float32) + gate[:, columns] * branch
        ).astype(jnp.bfloat16)
        shift_copy(c, part).start()

    def right_sent(slot, carry):
        @pl.when((slot <= me) & (me < used))
        def _():
            for copy in to_right(slot):
                copy.wait_send()

        return carry

    def row_step(c, carry):
        rows = pl.ds(pl.multiple_of(c * chunk, chunk), chunk)

        def last_slot_head(h, inner):
            columns = pl.ds(pl.multiple_of(h * HD, HD), HD)
            summed, weight_sum, top = with_slot(final, h, rows)
            attended[:, columns] = (summed / weight_sum).astype(jnp.bfloat16)
            return inner

        lax.fori_loop(0, heads, last_slot_head, 0)

        def project(owner, part):
            columns = pl.ds(pl.multiple_of(owner * width + part * part_width, HD), part_width)
            return jnp.dot(
                attended[...], weight[:, columns], preferred_element_type=jnp.float32
            ).astype(jnp.bfloat16)

        for part in range(column_parts):
            unit = c * column_parts + part
            for d in range(1, tensors):
                partial_out[d - 1, unit] = project(lax.rem(group + d, tensors), part)
                partial_copy(d, unit).start()
            partial_own[unit] = project(group, part)
            if part == lag:
                @pl.when(c == 0)
                def _():
                    lax.fori_loop(0, used, right_sent, 0)

            if part >= lag:
                combine(c, part - lag)
            else:

                @pl.when(c >= 1)
                def _():
                    combine(c - 1, column_parts + part - lag)

        return carry

    lax.fori_loop(0, row_chunks, row_step, 0)
    for part in range(column_parts - lag, column_parts):
        combine(row_chunks - 1, part)

    for copy in frame_copies:
        copy.wait_send()

    def slot_sent(slot, carry):
        @pl.when((slot >= me) & (me >= 1))
        def _():
            for copy in to_left(slot):
                copy.wait_send()

        for copy in to_pair(slot):
            copy.wait_send()
        return carry

    lax.fori_loop(0, used, slot_sent, 0)

    def chunk_done(c, carry):
        for part in range(column_parts):
            for d in range(1, tensors):
                partial_copy(d, c * column_parts + part).wait_send()
            shift_copy(c, part).wait()
        return carry

    lax.fori_loop(0, row_chunks, chunk_done, 0)


def on_device(
    hidden_state,
    frame_query,
    frame_key,
    frame_value,
    cache_key,
    cache_value,
    out_weight,
    level_gate,
    noise_level,
    frame_position,
    cached_count,
):
    sections = lax.axis_size("section")
    tensors = lax.axis_size("tensor")
    tokens, inner = frame_query.shape[1:]
    heads = inner // HD
    width = hidden_state.shape[2]
    used_rows = (sections - 1) * 2 * cache_key.shape[0]
    units = row_chunks * column_parts
    chunk = tokens // row_chunks
    piece = (chunk, width // column_parts)
    bf16, f32 = jnp.bfloat16, jnp.float32
    scalars = pl.BlockSpec(memory_space=pltpu.SMEM)
    near = pl.BlockSpec(memory_space=pltpu.VMEM)
    far = pl.BlockSpec(memory_space=pl.ANY)
    dma = pltpu.SemaphoreType.DMA
    return pl.pallas_call(
        functools.partial(kernel, sections, tensors),
        out_shape=jax.ShapeDtypeStruct(hidden_state.shape, bf16),
        in_specs=[scalars] * 3 + [near] * 6 + [far] * 2,
        out_specs=far,
        scratch_shapes=[
            pltpu.VMEM((tokens, inner), bf16),
            pltpu.VMEM((tokens, inner), bf16),
            pltpu.VMEM((used_rows, inner), bf16),
            pltpu.VMEM((used_rows, inner), bf16),
            pltpu.VMEM(out_weight.shape, bf16),
            pltpu.VMEM((tokens, width), bf16),
            pltpu.VMEM((heads, tokens, 2 * HD), f32),
            pltpu.VMEM((heads, tokens, HD), f32),
            pltpu.VMEM((1, width), f32),
            pltpu.VMEM((chunk, inner), bf16),
            pltpu.VMEM((tensors - 1, units) + piece, bf16),
            pltpu.VMEM((tensors - 1, units) + piece, bf16),
            pltpu.VMEM((units,) + piece, bf16),
            pltpu.VMEM((units,) + piece, bf16),
            dma((2,)),
            dma((2,)),
            dma((2,)),
            dma((2, sections - 1)),
            dma((2, sections - 1)),
            dma((2, sections - 1)),
            dma((2, sections - 1)),
            dma((2, sections - 1)),
            dma((tensors - 1, units)),
            dma((tensors - 1, units)),
            dma((units,)),
            dma((units,)),
        ],
        compiler_params=pltpu.CompilerParams(
            collective_id=0, has_side_effects=True, vmem_limit_bytes=60 * 1024 * 1024
        ),
    )(
        noise_level,
        frame_position,
        cached_count,
        frame_query[0],
        frame_key[0],
        frame_value[0],
        cache_key,
        cache_value,
        level_gate,
        out_weight,
        hidden_state,
    )


def solution(mesh):
    placed = (
        P(("parts", "section"), "seq", "tensor"),
        P(("parts", "section"), "seq", "tensor"),
        P(("parts", "section"), "seq", "tensor"),
        P(("parts", "section"), "seq", "tensor"),
        P(("parts", "section", "seq"), "tensor"),
        P(("parts", "section", "seq"), "tensor"),
        P("tensor", None),
        P(None, "tensor"),
        P("parts"),
        P("parts"),
        P("parts"),
    )
    return jax.shard_map(
        on_device,
        mesh=mesh,
        in_specs=placed,
        out_specs=P(("parts", "section"), "seq", "tensor"),
        check_vma=False,
    )
```
